768 devices in a mesh: dp: 96 (over y_hi, z, core), ep: 8 (over x, y_lo).
Axes of the slice: x: 4, y: 8 (y_hi: 4, y_lo: 2; y = y_hi * 2 + y_lo), z: 12, core: 2. Of those that a mesh axis runs over, the one named last changes fastest.
Arguments:
- grad_out: bfloat16 [12288, 6144], P('dp', 'ep'), may hold values from -6 to 6
- expert_ids: int32 [12288, 4], P('dp'), may hold values from 0 to 15, all different within a row
- route_probs: float32 [12288, 4], P('dp'), may hold values from 0.1 to 0.9
- saved_inputs: bfloat16 [1536, 6144], P(None, 'ep'), may hold values from -6 to 6
- w_gate: bfloat16 [10752, 6144], P('dp', 'ep'), may hold values from -0.078125 to 0.078125
- w_up: bfloat16 [10752, 6144], P('dp', 'ep'), may hold values from -0.078125 to 0.078125
- w_down: bfloat16 [10752, 6144], P('dp', 'ep'), may hold values from -0.3125 to 0.3125
Outputs:
- grad_in: bfloat16 [12288, 6144], P('dp', 'ep')
- grad_gate: float32 [10752, 6144], P('dp', 'ep')
- grad_up: float32 [10752, 6144], P('dp', 'ep')
- grad_down: float32 [10752, 6144], P('dp', 'ep')
The draws below stay inside these ranges and needn't reach their ends.
All inputs are finite; a program needn't handle non-finite values.
Results may differ from the reference program's by a relative error of at most 0.012.
Values may be sent and summed in bfloat16 or wider, within the bound.
No kernel may reach another device: no remote copies, remote signals or barrier semaphores. Data moves between devices by JAX's collectives and lax.ppermute only.
A program may use at most 32 MiB of HBM per device.

```python
import jax
import jax.numpy as jnp
from jax import lax

D = 6144
HID = 10752
EXPERTS = 16
TOP = 4
TOK_DEV = 128
CAP = 16
TOKENS = 12288
SLOTS = 1536
N_DP = 96


def level_of(key, dims, cuts, low, top_value):
    factor_of = 1.0
    for dim, blocks in cuts:
        draws = jax.random.uniform(jax.random.fold_in(jax.random.fold_in(key, 6), dim), (blocks,), jnp.float32, low / len(cuts), top_value / len(cuts))
        factor_of = factor_of * jnp.repeat(jnp.exp(draws), dims[dim] // blocks).reshape((-1,) + (1,) * (len(dims) - 1 - dim))
    return factor_of


def choose_distinct(key, rows, number_of, top, lift):
    ranking = jax.random.permutation(jax.random.fold_in(key, 1), number_of)
    pull = ranking
    for power in range(3):
        pull = pull * pull // number_of
    pull = pull * lift // number_of
    lots = jax.random.randint(jax.random.fold_in(key, 2), (rows, number_of), 0, 4096) + pull
    fixed_rows = jax.random.permutation(jax.random.fold_in(key, 3), rows)[jnp.arange(number_of) % rows]
    lots = jnp.where(jnp.arange(rows)[:, None] == fixed_rows[None, :], 1 << 14, lots)
    priority = lots * number_of + jnp.arange(number_of)
    return lax.top_k(priority.astype(jnp.int32), top)[1].astype(jnp.int32)


def bell_draw(stream_key, dims, deviation, reach, pieces=(), kind=jnp.bfloat16):
    entries = jax.random.normal(stream_key, dims, jnp.float32) * deviation
    if len(pieces) > 0:
        entries = level_of(stream_key, dims, pieces, -0.22, 0.18) * entries
    return jnp.clip(entries, min=-reach, max=reach).astype(kind)


def setup_inputs(seed: int = 0) -> dict:
    keys = jax.random.split(jax.random.key(seed), 8)
    return {
        "grad_out": bell_draw(keys[0], (TOKENS, D), 1.0, 6.0, ((0, 96), (1, 8))),
        "expert_ids": choose_distinct(keys[1], TOKENS, EXPERTS, TOP, 2048),
        "route_probs": jnp.clip(0.1 + 0.79999997 * jax.random.uniform(keys[2], (TOKENS, TOP), jnp.float32) ** level_of(keys[2], (TOKENS, TOP), ((0, 96),), -0.2, 0.2), 0.1, 0.9),
        "saved_inputs": bell_draw(keys[3], (SLOTS, D), 1.0, 6.0, ((1, 8),)),
        "w_gate": bell_draw(keys[4], (HID, D), D ** -0.5, 0.078125, ((0, 96), (1, 8))),
        "w_up": bell_draw(keys[5], (HID, D), D ** -0.5, 0.078125, ((0, 96), (1, 8))),
        "w_down": bell_draw(keys[6], (HID, D), (D // 16) ** -0.5, 0.3125, ((0, 96), (1, 8))),
    }


def route_block(routes, chances, capacity):
    matches = routes == 0
    chosen = jnp.any(matches, axis=1).astype(jnp.int32)
    weight = jnp.sum(jnp.where(matches, chances, jnp.zeros_like(chances)), axis=1)
    earlier = (jnp.cumsum(chosen) - chosen).astype(jnp.int32)
    retained = (chosen > 0) & (earlier < capacity)
    placement = ((earlier[None, :] == jnp.arange(capacity, dtype=jnp.int32)[:, None]) & retained[None, :]).astype(jnp.float32)
    return placement, weight


def reference(grad_out, expert_ids, route_probs, saved_inputs, w_gate, w_up, w_down):
    routes = expert_ids.reshape(N_DP, TOK_DEV, TOP)
    chances = route_probs.reshape(N_DP, TOK_DEV, TOP)
    placement, weight = jax.vmap(lambda a, b: route_block(a, b, CAP))(routes, chances)
    blocks = grad_out.reshape(N_DP, TOK_DEV, D).astype(jnp.float32)
    weighted = weight[:, :, None] * blocks
    out_grad = jnp.einsum("pct,ptd->pcd", placement, weighted, precision=lax.Precision.HIGHEST).astype(jnp.bfloat16).reshape(SLOTS, D)
    gate_pre = jnp.dot(saved_inputs, w_gate.T, preferred_element_type=jnp.float32)
    up_pre = jnp.dot(saved_inputs, w_up.T, preferred_element_type=jnp.float32)
    sigmoid_gate = jax.nn.sigmoid(gate_pre)
    activated = gate_pre * sigmoid_gate
    hidden = (activated * up_pre).astype(jnp.bfloat16)
    hid_grad = jnp.dot(out_grad, w_down.T, preferred_element_type=jnp.float32)
    gate_slope = sigmoid_gate + gate_pre * sigmoid_gate * (1.0 - sigmoid_gate)
    gate_grad = (hid_grad * up_pre * gate_slope).astype(jnp.bfloat16)
    up_grad = (hid_grad * activated).astype(jnp.bfloat16)
    slot_grad = (jnp.dot(gate_grad, w_gate, preferred_element_type=jnp.float32)
                 + jnp.dot(up_grad, w_up, preferred_element_type=jnp.float32)).astype(jnp.bfloat16)
    grad_gate = jnp.dot(gate_grad.T, saved_inputs, preferred_element_type=jnp.float32)
    grad_up = jnp.dot(up_grad.T, saved_inputs, preferred_element_type=jnp.float32)
    grad_down = jnp.dot(hidden.T, out_grad, preferred_element_type=jnp.float32)
    routed = jnp.einsum("pct,pcd->ptd", placement, slot_grad.reshape(N_DP, CAP, D).astype(jnp.float32), precision=lax.Precision.HIGHEST)
    grad_in = (blocks + routed).astype(jnp.bfloat16).reshape(TOKENS, D)
    return grad_in, grad_gate, grad_up, grad_down
```

```python
import jax
import jax.numpy as jnp
from jax import lax
from jax.sharding import Mesh, PartitionSpec as P

AXES = ("yh", "zh", "zl", "core", "x", "yl")
SIZES = (4, 6, 2, 2, 4, 2)
DP = AXES[:4]
EP = AXES[4:]
FAR = ("yh", "zh")
N_FAR = 24
N_EP = 8
SWAP = [(0, 1), (1, 0)]


def route_block(routes, chances, capacity):
    matches = routes == 0
    chosen = jnp.any(matches, axis=1).astype(jnp.int32)
    weight = jnp.sum(jnp.where(matches, chances, jnp.zeros_like(chances)), axis=1)
    earlier = jnp.cumsum(chosen) - chosen
    retained = (chosen > 0) & (earlier < capacity)
    placement = (
        (earlier[None, :] == jnp.arange(capacity, dtype=jnp.int32)[:, None]) & retained[None, :]
    ).astype(jnp.float32)
    return (placement, weight)


def spread(value, axes, n):
    copies = jnp.broadcast_to(value[None], (n,) + value.shape)
    return lax.all_to_all(copies, axes, 0, 0, tiled=True)


def local(grad_out, expert_ids, route_probs, saved_inputs, w_gate, w_up, w_down):
    capacity = grad_out.shape[0] // 8
    units, width = w_gate.shape
    slots = N_FAR * capacity
    share = 4 * units // N_EP

    own = jnp.stack([w_gate, w_up, w_down])
    near = lax.ppermute(own, "core", SWAP)
    across = lax.ppermute(own, "zl", SWAP)
    diagonal = lax.ppermute(across, "core", SWAP)
    weights = jnp.stack([own, near, across, diagonal], axis=1).reshape(3, 4 * units, width)

    placement, weight = route_block(expert_ids, route_probs, capacity)
    residual = grad_out.astype(jnp.float32)
    weighted = weight[:, None] * residual
    outgoing = jnp.dot(placement, weighted, precision=lax.Precision.HIGHEST).astype(jnp.bfloat16)
    gathered = spread(spread(outgoing, "zh", 6).reshape(6 * capacity, width), "yh", 4).reshape(slots, width)

    member = lax.axis_index("zl") * 2 + lax.axis_index("core")
    saved = lax.dynamic_index_in_dim(
        saved_inputs.reshape(N_FAR, 4, capacity, width), member, axis=1, keepdims=False
    ).reshape(slots, width)

    dims = (((1,), (1,)), ((), ()))
    gate_part = lax.dot_general(weights[0], saved, dims, preferred_element_type=jnp.float32)
    up_part = lax.dot_general(weights[1], saved, dims, preferred_element_type=jnp.float32)
    hid_part = lax.dot_general(weights[2], gathered, dims, preferred_element_type=jnp.float32)
    parts = jnp.stack(
        [p.astype(jnp.bfloat16).reshape(N_EP, share, slots) for p in (gate_part, up_part, hid_part)], axis=1
    )
    parts = lax.all_to_all(parts, EP, 0, 0, tiled=True)
    gate_pre, up_pre, hid_grad = jnp.sum(parts.astype(jnp.float32), axis=0)

    sigmoid_gate = jax.nn.sigmoid(gate_pre)
    activated = gate_pre * sigmoid_gate
    hidden = (activated * up_pre).astype(jnp.bfloat16)
    gate_slope = sigmoid_gate + gate_pre * sigmoid_gate * (1.0 - sigmoid_gate)
    gate_grad = (hid_grad * up_pre * gate_slope).astype(jnp.bfloat16)
    up_grad = (hid_grad * activated).astype(jnp.bfloat16)
    whole = spread(jnp.stack([gate_grad, up_grad, hidden]), EP, N_EP)
    gate_grad, up_grad, hidden = [whole[:, k].reshape(4 * units, slots) for k in range(3)]

    grads = jnp.stack(
        [
            jnp.dot(gate_grad, saved, preferred_element_type=jnp.float32),
            jnp.dot(up_grad, saved, preferred_element_type=jnp.float32),
            jnp.dot(hidden, gathered, preferred_element_type=jnp.float32),
        ]
    ).reshape(3, 4, units, width)
    from_near = lax.ppermute(grads[:, 1::2].astype(jnp.bfloat16), "core", SWAP)

    dims = (((0,), (0,)), ((), ()))
    slot_part = lax.dot_general(gate_grad, weights[0], dims, preferred_element_type=jnp.float32) + lax.dot_general(
        up_grad, weights[1], dims, preferred_element_type=jnp.float32
    )
    half = grads[:, 0::2] + from_near.astype(jnp.float32)
    from_across = lax.ppermute(half[:, 1].astype(jnp.bfloat16), "zl", SWAP)

    slot_part = slot_part.astype(jnp.bfloat16).reshape(4, 6 * capacity, width)
    slot_part = jnp.sum(lax.all_to_all(slot_part, "yh", 0, 0, tiled=True).astype(jnp.float32), axis=0)
    slot_part = slot_part.astype(jnp.bfloat16).reshape(6, capacity, width)
    own_slots = jnp.sum(lax.all_to_all(slot_part, "zh", 0, 0, tiled=True).astype(jnp.float32), axis=0)
    own_slots = own_slots.astype(jnp.bfloat16)

    grad_gate, grad_up, grad_down = half[:, 0] + from_across.astype(jnp.float32)
    routed = jnp.dot(placement.T, own_slots.astype(jnp.float32), precision=lax.Precision.HIGHEST)
    grad_in = (residual + routed).astype(jnp.bfloat16)
    return (grad_in, grad_gate, grad_up, grad_down)


def solution(mesh):
    fine = Mesh(mesh.devices.reshape(SIZES), AXES)
    in_specs = (P(DP, EP), P(DP, None), P(DP, None), P(None, EP), P(DP, EP), P(DP, EP), P(DP, EP))
    return jax.shard_map(local, mesh=fine, in_specs=in_specs, out_specs=(P(DP, EP),) * 4, check_vma=False)
```

```python
import functools

import jax
import jax.numpy as jnp
from jax import lax
from jax.experimental import pallas as pl
from jax.experimental.pallas import tpu as pltpu
from jax.sharding import Mesh, PartitionSpec as P

AXES = ("yh", "zh", "zl", "core", "x", "yl")
SIZES = (4, 6, 2, 2, 4, 2)
DP = AXES[:4]
EP = AXES[4:]
N_YH = 4
N_ZH = 6
N_FAR = 24
N_EP = 8
SWAP = [(0, 1), (1, 0)]
BF16 = jnp.bfloat16
F32 = jnp.float32


VMEM = pltpu.VMEM
HBM = pltpu.HBM


def scratch_call(body, outs, scratch, flops, *args):
    moved = sum(a.size * a.dtype.itemsize for a in args)
    return pl.pallas_call(
        body,
        out_shape=outs,
        in_specs=[pl.BlockSpec(memory_space=VMEM)] * len(args),
        out_specs=[pl.BlockSpec(memory_space=VMEM)] * len(outs),
        scratch_shapes=[VMEM(scratch, BF16)],
        cost_estimate=pl.CostEstimate(flops=flops, bytes_accessed=moved, transcendentals=0),
        compiler_params=pltpu.CompilerParams(vmem_limit_bytes=24 * 1024 * 1024),
    )(*args)


def kernel_call(body, outs, flops, *args):
    moved = sum(a.size * a.dtype.itemsize for a in args)
    return pl.pallas_call(
        body,
        out_shape=outs,
        in_specs=[pl.BlockSpec(memory_space=VMEM)] * len(args),
        out_specs=[pl.BlockSpec(memory_space=VMEM)] * len(outs),
        cost_estimate=pl.CostEstimate(flops=flops, bytes_accessed=moved, transcendentals=0),
        compiler_params=pltpu.CompilerParams(vmem_limit_bytes=24 * 1024 * 1024),
    )(*args)


def array(*shape, dtype=BF16):
    return jax.ShapeDtypeStruct(shape, dtype)


def dot(a, b, dims):
    return lax.dot_general(a, b, (dims, ((), ())), preferred_element_type=F32)


ROWS = ((0,), (0,))
PLAIN = ((1,), (0,))
LANES = ((1,), (1,))


def route_kernel(
    grad_hbm, ids_hbm, probs_hbm, wg_hbm, wu_hbm, wd_hbm, copies_ref, placement_ref, own_ref, grad_ref, ids_ref, probs_ref, sems
):
    pairs = (
        (ids_hbm, ids_ref),
        (probs_hbm, probs_ref),
        (grad_hbm, grad_ref),
        (wg_hbm, own_ref.at[0]),
        (wu_hbm, own_ref.at[1]),
        (wd_hbm, own_ref.at[2]),
    )
    moves = [pltpu.make_async_copy(a, b, sems.at[i]) for i, (a, b) in enumerate(pairs)]
    for move in moves:
        move.start()
    tokens = grad_ref.shape[0]
    copies, capacity, _ = copies_ref.shape
    rows = lax.broadcasted_iota(jnp.int32, (tokens, tokens), 0)
    columns = lax.broadcasted_iota(jnp.int32, (tokens, tokens), 1)
    before = jnp.where(rows < columns, 1.0, 0.0).astype(BF16)
    slot = lax.broadcasted_iota(jnp.int32, (capacity, tokens), 0).astype(F32)
    moves[0].wait()
    moves[1].wait()
    matches = ids_ref[...] == 0
    chosen = jnp.max(jnp.where(matches, 1.0, 0.0), axis=0, keepdims=True)
    weight = jnp.sum(jnp.where(matches, probs_ref[...], 0.0), axis=0, keepdims=True)
    chosen = jnp.broadcast_to(chosen, (capacity, tokens))
    earlier = dot(chosen.astype(BF16), before, PLAIN)
    placement = jnp.where((earlier == slot) & (chosen > 0.5), 1.0, 0.0)
    placement_ref[...] = placement.astype(BF16)
    scale = jnp.sum(placement * weight, axis=1, keepdims=True)
    moves[2].wait()
    picked = dot(placement.astype(BF16), grad_ref[...], PLAIN)
    outgoing = (picked * scale).astype(BF16)
    for i in range(copies):
        copies_ref[i] = outgoing
    for move in moves[3:]:
        move.wait()


def copies_kernel(value_ref, copies_ref):
    for i in range(copies_ref.shape[0]):
        copies_ref[i] = value_ref[...]


def pre_kernel(own_ref, across_ref, near_ref, diagonal_ref, saved_ref, gathered_ref, parts_ref, w_ref):
    units = own_ref.shape[1]
    group = 4 * units
    for k in range(3):
        for i, ref in enumerate((own_ref, across_ref, near_ref, diagonal_ref)):
            w_ref[k * group + i * units : k * group + (i + 1) * units] = ref[k]
    parts_ref[:, : 2 * group] = dot(saved_ref[...], w_ref[: 2 * group], LANES).astype(BF16)
    parts_ref[:, 2 * group :] = dot(gathered_ref[...], w_ref[2 * group :], LANES).astype(BF16)


def activation_kernel(parts_ref, copies_ref):
    sources, _, wide = parts_ref.shape
    group = wide // 3
    total = parts_ref[0].astype(F32)
    for i in range(1, sources):
        total += parts_ref[i].astype(F32)
    gate_pre, up_pre, hid_grad = (total[:, k * group : (k + 1) * group] for k in range(3))
    sigmoid_gate = jax.nn.sigmoid(gate_pre)
    activated = gate_pre * sigmoid_gate
    gate_slope = sigmoid_gate + gate_pre * sigmoid_gate * (1.0 - sigmoid_gate)
    gate_grad = hid_grad * up_pre * gate_slope
    act = jnp.concatenate([gate_grad, hid_grad * activated, activated * up_pre], axis=1).astype(BF16)
    for i in range(sources):
        copies_ref[i] = act


def weight_grads(act_ref, saved_ref, gathered_ref, k, half):
    group = act_ref.shape[1] // 3
    start = k * group + half * group // 2
    low = start // 128 * 128
    high = min((start + group // 2 + 127) // 128 * 128, 3 * group)
    part = dot(act_ref[:, low:high], (gathered_ref if k == 2 else saved_ref)[...], ROWS)
    return part[start - low : start - low + group // 2]


def slot_kernel(
    act_ref, saved_ref, gathered_ref, own, across, near, diagonal, slot_hbm, sent_hbm, w_ref, slot_ref, sent_ref, in_sems, out_sems
):
    units = own.shape[1]
    group = 4 * units
    fetches = []
    for k in range(2):
        for i, piece in enumerate((own, across, near, diagonal)):
            place = w_ref.at[pl.ds(k * group + i * units, units)]
            fetches.append(pltpu.make_async_copy(piece.at[k], place, in_sems.at[4 * k + i]))
    for fetch in fetches:
        fetch.start()
    stores = []
    for k in range(3):
        sent_ref[k] = weight_grads(act_ref, saved_ref, gathered_ref, k, 1).astype(BF16)
        stores.append(pltpu.make_async_copy(sent_ref.at[k], sent_hbm.at[k], out_sems.at[k]))
        stores[k].start()
    for fetch in fetches:
        fetch.wait()
    slot_ref[...] = dot(act_ref[:, : 2 * group], w_ref[...], PLAIN).astype(BF16)
    stores.append(pltpu.make_async_copy(slot_ref, slot_hbm, out_sems.at[3]))
    stores[3].start()
    for store in stores:
        store.wait()


def kept_kernel(act_ref, saved_ref, gathered_ref, near_ref, own_ref, sent_ref):
    units = own_ref.shape[1]
    for k in range(3):
        part = weight_grads(act_ref, saved_ref, gathered_ref, k, 0)
        own_ref[k] = part[:units] + near_ref[k, :units].astype(F32)
        sent_ref[k] = (part[units:] + near_ref[k, units:].astype(F32)).astype(BF16)


def sum_kernel(parts_ref, total_ref):
    total = parts_ref[0].astype(F32)
    for i in range(1, parts_ref.shape[0]):
        total += parts_ref[i].astype(F32)
    total_ref[...] = total.astype(BF16)


def result_kernel(parts_ref, placement_ref, grad_ref, result_ref):
    total = parts_ref[0].astype(F32)
    for i in range(1, parts_ref.shape[0]):
        total += parts_ref[i].astype(F32)
    routed = dot(placement_ref[...], total.astype(BF16), ROWS)
    result_ref[...] = (grad_ref[...].astype(F32) + routed).astype(BF16)


def local(grad_out, expert_ids, route_probs, saved_inputs, w_gate, w_up, w_down):
    tokens, width = grad_out.shape
    capacity = tokens // 8
    units = w_gate.shape[0]
    slots = N_FAR * capacity
    group = 4 * units

    copies, placement, own = pl.pallas_call(
        route_kernel,
        out_shape=[array(N_ZH, capacity, width), array(capacity, tokens), HBM((3, units, width), BF16)],
        in_specs=[pl.BlockSpec(memory_space=pl.ANY)] * 6,
        out_specs=[pl.BlockSpec(memory_space=VMEM)] * 3,
        scratch_shapes=[
            VMEM((tokens, width), BF16),
            VMEM(expert_ids.shape[::-1], jnp.int32),
            VMEM(route_probs.shape[::-1], F32),
            pltpu.SemaphoreType.DMA((6,)),
        ],
    )(grad_out, expert_ids.T, route_probs.T, w_gate, w_up, w_down)

    copies = lax.all_to_all(copies, "zh", 0, 0, tiled=True).reshape(N_ZH * capacity, width)
    copies, own = lax.optimization_barrier((copies, own))
    near = lax.ppermute(own, "core", SWAP)
    across = lax.ppermute(own, "zl", SWAP)
    (copies,) = kernel_call(copies_kernel, [HBM((N_YH, N_ZH * capacity, width), BF16)], 0, copies)
    diagonal = lax.ppermute(across, "core", SWAP)
    gathered = lax.all_to_all(copies, "yh", 0, 0, tiled=True).reshape(slots, width)

    member = lax.axis_index("zl") * 2 + lax.axis_index("core")
    saved = lax.dynamic_index_in_dim(
        saved_inputs.reshape(N_FAR, 4, capacity, width), member, axis=1, keepdims=False
    ).reshape(slots, width)

    pieces = (own, across, near, diagonal)
    (parts,) = scratch_call(
        pre_kernel, [array(slots, 3 * group)], (3 * group, width), 6 * slots * group * width, *pieces, saved, gathered
    )
    parts = lax.all_to_all(parts.reshape(N_EP, slots // N_EP, 3 * group), EP, 0, 0, tiled=True)
    (copies,) = kernel_call(activation_kernel, [array(*parts.shape)], 20 * parts.size, parts)
    act = lax.all_to_all(copies, EP, 0, 0, tiled=True)
    act = act.reshape(slots, 3 * group)

    slot_part, sent = pl.pallas_call(
        slot_kernel,
        out_shape=[HBM((slots, width), BF16), HBM((3, 2 * units, width), BF16)],
        in_specs=[pl.BlockSpec(memory_space=VMEM)] * 3 + [pl.BlockSpec(memory_space=pl.ANY)] * 4,
        out_specs=[pl.BlockSpec(memory_space=pl.ANY)] * 2,
        scratch_shapes=[
            VMEM((2 * group, width), BF16),
            VMEM((slots, width), BF16),
            VMEM((3, 2 * units, width), BF16),
            pltpu.SemaphoreType.DMA((8,)),
            pltpu.SemaphoreType.DMA((4,)),
        ],
        cost_estimate=pl.CostEstimate(flops=7 * slots * group * width, bytes_accessed=6000000, transcendentals=0),
        compiler_params=pltpu.CompilerParams(vmem_limit_bytes=24 * 1024 * 1024),
    )(act, saved, gathered, *pieces)

    from_near = lax.ppermute(sent, "core", SWAP)
    slot_part = lax.all_to_all(slot_part.reshape(N_YH, N_ZH * capacity, width), "yh", 0, 0, tiled=True)
    kept, sent = kernel_call(
        kept_kernel,
        [HBM((3, units, width), F32), HBM((3, units, width), BF16)],
        6 * slots * group * width,
        act,
        saved,
        gathered,
        from_near,
    )
    from_across = lax.ppermute(sent, "zl", SWAP)
    (slot_part,) = kernel_call(sum_kernel, [HBM((N_ZH * capacity, width), BF16)], slot_part.size, slot_part)
    slot_part, from_across = lax.optimization_barrier((slot_part, from_across))
    slot_part = lax.all_to_all(slot_part.reshape(N_ZH, capacity, width), "zh", 0, 0, tiled=True)
    (grad_in,) = kernel_call(result_kernel, [array(tokens, width)], tokens * width * 32, slot_part, placement, grad_out)

    grad_gate, grad_up, grad_down = [kept[k] + from_across[k].astype(F32) for k in range(3)]
    return (grad_in, grad_gate, grad_up, grad_down)


def solution(mesh):
    fine = Mesh(mesh.devices.reshape(SIZES), AXES)
    in_specs = (P(DP, EP), P(DP, None), P(DP, None), P(None, EP), P(DP, EP), P(DP, EP), P(DP, EP))
    return jax.shard_map(local, mesh=fine, in_specs=in_specs, out_specs=(P(DP, EP),) * 4, check_vma=False)
```

```python
import functools

import jax
import jax.numpy as jnp
from jax import lax
from jax.experimental import pallas as pl
from jax.experimental.pallas import tpu as pltpu
from jax.sharding import Mesh, PartitionSpec as P

AXES = ("yh", "zh", "zl", "core", "x", "yl")
SIZES = (4, 6, 2, 2, 4, 2)
DP = AXES[:4]
EP = AXES[4:]
N_YH = 4
N_ZH = 6
N_FAR = 24
N_EP = 8
SWAP = [(0, 1), (1, 0)]
BF16 = jnp.bfloat16
F32 = jnp.float32


VMEM = pltpu.VMEM
HBM = pltpu.HBM


def kernel_call(body, outs, flops, *args):
    moved = sum(a.size * a.dtype.itemsize for a in args)
    return pl.pallas_call(
        body,
        out_shape=outs,
        in_specs=[pl.BlockSpec(memory_space=VMEM)] * len(args),
        out_specs=[pl.BlockSpec(memory_space=VMEM)] * len(outs),
        cost_estimate=pl.CostEstimate(flops=flops, bytes_accessed=moved, transcendentals=0),
        compiler_params=pltpu.CompilerParams(vmem_limit_bytes=24 * 1024 * 1024),
    )(*args)


def array(*shape, dtype=BF16):
    return jax.ShapeDtypeStruct(shape, dtype)


def dot(a, b, dims):
    return lax.dot_general(a, b, (dims, ((), ())), preferred_element_type=F32)


ROWS = ((0,), (0,))
PLAIN = ((1,), (0,))
LANES = ((1,), (1,))


def route_kernel(
    grad_hbm, ids_hbm, probs_hbm, wg_hbm, wu_hbm, wd_hbm, copies_ref, placement_ref, own_ref, grad_ref, ids_ref, probs_ref, sems
):
    pairs = (
        (ids_hbm, ids_ref),
        (probs_hbm, probs_ref),
        (grad_hbm, grad_ref),
        (wg_hbm, own_ref.at[0]),
        (wu_hbm, own_ref.at[1]),
        (wd_hbm, own_ref.at[2]),
    )
    moves = [pltpu.make_async_copy(a, b, sems.at[i]) for i, (a, b) in enumerate(pairs)]
    for move in moves:
        move.start()
    tokens = grad_ref.shape[0]
    copies, capacity, _ = copies_ref.shape
    rows = lax.broadcasted_iota(jnp.int32, (tokens, tokens), 0)
    columns = lax.broadcasted_iota(jnp.int32, (tokens, tokens), 1)
    before = jnp.where(rows < columns, 1.0, 0.0).astype(BF16)
    slot = lax.broadcasted_iota(jnp.int32, (capacity, tokens), 0).astype(F32)
    moves[0].wait()
    moves[1].wait()
    matches = ids_ref[...] == 0
    chosen = jnp.max(jnp.where(matches, 1.0, 0.0), axis=0, keepdims=True)
    weight = jnp.sum(jnp.where(matches, probs_ref[...], 0.0), axis=0, keepdims=True)
    chosen = jnp.broadcast_to(chosen, (capacity, tokens))
    earlier = dot(chosen.astype(BF16), before, PLAIN)
    placement = jnp.where((earlier == slot) & (chosen > 0.5), 1.0, 0.0)
    placement_ref[...] = placement.astype(BF16)
    scale = jnp.sum(placement * weight, axis=1, keepdims=True)
    moves[2].wait()
    picked = dot(placement.astype(BF16), grad_ref[...], PLAIN)
    outgoing = (picked * scale).astype(BF16)
    for i in range(copies):
        copies_ref[i] = outgoing
    for move in moves[3:]:
        move.wait()


def copies_kernel(value_ref, copies_ref):
    for i in range(copies_ref.shape[0]):
        copies_ref[i] = value_ref[...]


def pre_kernel(own_ref, across_ref, near_ref, diagonal_ref, saved_ref, gathered_ref, parts_ref, w_hbm, w_ref, sem):
    units = own_ref.shape[1]
    group = 4 * units
    for k in range(3):
        for i, ref in enumerate((own_ref, across_ref, near_ref, diagonal_ref)):
            w_ref[k * group + i * units : k * group + (i + 1) * units] = ref[k]
    store = pltpu.make_async_copy(w_ref.at[pl.ds(0, 2 * group)], w_hbm, sem.at[0])
    store.start()
    parts_ref[:, : 2 * group] = dot(saved_ref[...], w_ref[: 2 * group], LANES).astype(BF16)
    parts_ref[:, 2 * group :] = dot(gathered_ref[...], w_ref[2 * group :], LANES).astype(BF16)
    store.wait()


def activation_kernel(parts_ref, copies_ref):
    sources, _, wide = parts_ref.shape
    group = wide // 3
    total = parts_ref[0].astype(F32)
    for i in range(1, sources):
        total += parts_ref[i].astype(F32)
    gate_pre, up_pre, hid_grad = (total[:, k * group : (k + 1) * group] for k in range(3))
    sigmoid_gate = jax.nn.sigmoid(gate_pre)
    activated = gate_pre * sigmoid_gate
    gate_slope = sigmoid_gate + gate_pre * sigmoid_gate * (1.0 - sigmoid_gate)
    gate_grad = hid_grad * up_pre * gate_slope
    act = jnp.concatenate([gate_grad, hid_grad * activated, activated * up_pre], axis=1).astype(BF16)
    for i in range(sources):
        copies_ref[i] = act


def columns_of(act_ref, k, members):
    group = act_ref.shape[1] // 3
    units = group // 4
    return [act_ref[:, k * group + i * units : k * group + (i + 1) * units] for i in members]


def slot_kernel(act_ref, w_ref, slot_hbm, sent_hbm, slot_ref, sent_ref, out_sems):
    group = w_ref.shape[0] // 2
    units = group // 4
    columns = [c for k in range(3) for c in columns_of(act_ref, k, (1, 3))]
    spare = sent_ref.shape[1] - 6 * units
    columns.append(jnp.zeros((act_ref.shape[0], spare), BF16))
    sent_ref[...] = jnp.concatenate(columns, axis=1)
    sent_store = pltpu.make_async_copy(sent_ref, sent_hbm, out_sems.at[0])
    sent_store.start()
    stores = [sent_store]
    rows = act_ref.shape[0] // N_YH
    for i in range(N_YH):
        block = pl.ds(i * rows, rows)
        slot_ref[block] = dot(act_ref[block, : 2 * group], w_ref[...], PLAIN).astype(BF16)
        stores.append(pltpu.make_async_copy(slot_ref.at[block], slot_hbm.at[block], out_sems.at[1 + i]))
        stores[-1].start()
    for store in stores:
        store.wait()


def kept_kernel(act_ref, act_far_ref, saved_ref, saved_far_ref, gathered_ref, gathered_far_ref, own_ref, sent_ref):
    units = own_ref.shape[1]
    for k in range(3):
        here, far = (gathered_ref, gathered_far_ref) if k == 2 else (saved_ref, saved_far_ref)
        part = dot(jnp.concatenate(columns_of(act_ref, k, (0, 2)), axis=1), here[...], ROWS)
        part += dot(act_far_ref[:, 2 * k * units : 2 * (k + 1) * units], far[...], ROWS)
        own_ref[k] = part[:units]
        sent_ref[k] = part[units:].astype(BF16)


def sum_kernel(parts_ref, total_ref):
    total = parts_ref[0].astype(F32)
    for i in range(1, parts_ref.shape[0]):
        total += parts_ref[i].astype(F32)
    total_ref[...] = total.astype(BF16)


def result_kernel(parts_ref, placement_ref, grad_ref, result_ref):
    total = parts_ref[0].astype(F32)
    for i in range(1, parts_ref.shape[0]):
        total += parts_ref[i].astype(F32)
    routed = dot(placement_ref[...], total.astype(BF16), ROWS)
    result_ref[...] = (grad_ref[...].astype(F32) + routed).astype(BF16)


def local(grad_out, expert_ids, route_probs, saved_inputs, w_gate, w_up, w_down):
    tokens, width = grad_out.shape
    capacity = tokens // 8
    units = w_gate.shape[0]
    slots = N_FAR * capacity
    group = 4 * units

    copies, placement, own = pl.pallas_call(
        route_kernel,
        out_shape=[array(N_ZH, capacity, width), array(capacity, tokens), HBM((3, units, width), BF16)],
        in_specs=[pl.BlockSpec(memory_space=pl.ANY)] * 6,
        out_specs=[pl.BlockSpec(memory_space=VMEM)] * 3,
        scratch_shapes=[
            VMEM((tokens, width), BF16),
            VMEM(expert_ids.shape[::-1], jnp.int32),
            VMEM(route_probs.shape[::-1], F32),
            pltpu.SemaphoreType.DMA((6,)),
        ],
    )(grad_out, expert_ids.T, route_probs.T, w_gate, w_up, w_down)

    copies = lax.all_to_all(copies, "zh", 0, 0, tiled=True).reshape(N_ZH * capacity, width)
    copies, own = lax.optimization_barrier((copies, own))
    near = lax.ppermute(own, "core", SWAP)
    across = lax.ppermute(own, "zl", SWAP)
    (copies,) = kernel_call(copies_kernel, [HBM((N_YH, N_ZH * capacity, width), BF16)], 0, copies)
    diagonal = lax.ppermute(across, "core", SWAP)
    gathered = lax.all_to_all(copies, "yh", 0, 0, tiled=True).reshape(slots, width)

    def slots_of(member):
        rows = saved_inputs.reshape(N_FAR, 4, capacity, width)
        return lax.dynamic_index_in_dim(rows, member, axis=1, keepdims=False).reshape(slots, width)

    chip, core = lax.axis_index("zl"), lax.axis_index("core")
    saved = slots_of(chip * 2 + core)
    saved_far = slots_of((1 - chip) * 2 + core)

    pieces = (own, across, near, diagonal)
    parts, w_both = pl.pallas_call(
        pre_kernel,
        out_shape=[array(slots, 3 * group), HBM((2 * group, width), BF16)],
        in_specs=[pl.BlockSpec(memory_space=VMEM)] * 6,
        out_specs=[pl.BlockSpec(memory_space=VMEM), pl.BlockSpec(memory_space=pl.ANY)],
        scratch_shapes=[VMEM((3 * group, width), BF16), pltpu.SemaphoreType.DMA((1,))],
        cost_estimate=pl.CostEstimate(flops=6 * slots * group * width, bytes_accessed=4000000, transcendentals=0),
        compiler_params=pltpu.CompilerParams(vmem_limit_bytes=24 * 1024 * 1024),
    )(*pieces, saved, gathered)
    gathered_far = lax.ppermute(gathered, "zl", SWAP)
    parts = lax.all_to_all(parts.reshape(N_EP, slots // N_EP, 3 * group), EP, 0, 0, tiled=True)
    (copies,) = kernel_call(activation_kernel, [array(*parts.shape)], 20 * parts.size, parts)
    act = lax.all_to_all(copies, EP, 0, 0, tiled=True)
    act = act.reshape(slots, 3 * group)

    slot_part, sent = pl.pallas_call(
        slot_kernel,
        out_shape=[HBM((slots, width), BF16), HBM((slots, width), BF16)],
        in_specs=[pl.BlockSpec(memory_space=VMEM)] * 2,
        out_specs=[pl.BlockSpec(memory_space=pl.ANY)] * 2,
        scratch_shapes=[
            VMEM((slots, width), BF16),
            VMEM((slots, width), BF16),
            pltpu.SemaphoreType.DMA((1 + N_YH,)),
        ],
        cost_estimate=pl.CostEstimate(flops=4 * slots * group * width, bytes_accessed=6000000, transcendentals=0),
        compiler_params=pltpu.CompilerParams(vmem_limit_bytes=24 * 1024 * 1024),
    )(act, w_both)

    act_far = lax.ppermute(sent, "zl", SWAP)
    slot_part = lax.all_to_all(slot_part.reshape(N_YH, N_ZH * capacity, width), "yh", 0, 0, tiled=True)
    kept, sent = kernel_call(
        kept_kernel,
        [HBM((3, units, width), F32), HBM((3, units, width), BF16)],
        6 * slots * group * width,
        act,
        act_far,
        saved,
        saved_far,
        gathered,
        gathered_far,
    )
    from_near = lax.ppermute(sent, "core", SWAP)
    (slot_part,) = kernel_call(sum_kernel, [HBM((N_ZH * capacity, width), BF16)], slot_part.size, slot_part)
    slot_part = lax.all_to_all(slot_part.reshape(N_ZH, capacity, width), "zh", 0, 0, tiled=True)
    (grad_in,) = kernel_call(result_kernel, [array(tokens, width)], tokens * width * 32, slot_part, placement, grad_out)

    grad_gate, grad_up, grad_down = [kept[k] + from_near[k].astype(F32) for k in range(3)]
    return (grad_in, grad_gate, grad_up, grad_down)


def solution(mesh):
    fine = Mesh(mesh.devices.reshape(SIZES), AXES)
    in_specs = (P(DP, EP), P(DP, None), P(DP, None), P(None, EP), P(DP, EP), P(DP, EP), P(DP, EP))
    return jax.shard_map(local, mesh=fine, in_specs=in_specs, out_specs=(P(DP, EP),) * 4, check_vma=False)
```

```python
import functools

import jax
import jax.numpy as jnp
from jax import lax
from jax.experimental import pallas as pl
from jax.experimental.pallas import tpu as pltpu
from jax.sharding import Mesh, PartitionSpec as P

AXES = ("yh", "zh", "zl", "core", "x", "yl")
SIZES = (4, 6, 2, 2, 4, 2)
DP = AXES[:4]
EP = AXES[4:]
N_YH = 4
N_ZH = 6
N_FAR = 24
N_EP = 8
SWAP = [(0, 1), (1, 0)]
BF16 = jnp.bfloat16
F32 = jnp.float32


VMEM = pltpu.VMEM
HBM = pltpu.HBM


def kernel_call(body, outs, flops, *args):
    moved = sum(a.size * a.dtype.itemsize for a in args)
    return pl.pallas_call(
        body,
        out_shape=outs,
        in_specs=[pl.BlockSpec(memory_space=VMEM)] * len(args),
        out_specs=[pl.BlockSpec(memory_space=VMEM)] * len(outs),
        cost_estimate=pl.CostEstimate(flops=flops, bytes_accessed=moved, transcendentals=0),
        compiler_params=pltpu.CompilerParams(vmem_limit_bytes=24 * 1024 * 1024),
    )(*args)


def array(*shape, dtype=BF16):
    return jax.ShapeDtypeStruct(shape, dtype)


def dot(a, b, dims):
    return lax.dot_general(a, b, (dims, ((), ())), preferred_element_type=F32)


ROWS = ((0,), (0,))
PLAIN = ((1,), (0,))
LANES = ((1,), (1,))


def route_kernel(
    grad_hbm, ids_hbm, probs_hbm, wg_hbm, wu_hbm, wd_hbm, copies_ref, placement_ref, own_ref, grad_ref, ids_ref, probs_ref, sems
):
    pairs = (
        (ids_hbm, ids_ref),
        (probs_hbm, probs_ref),
        (grad_hbm, grad_ref),
        (wg_hbm, own_ref.at[0]),
        (wu_hbm, own_ref.at[1]),
        (wd_hbm, own_ref.at[2]),
    )
    moves = [pltpu.make_async_copy(a, b, sems.at[i]) for i, (a, b) in enumerate(pairs)]
    for move in moves:
        move.start()
    tokens = grad_ref.shape[0]
    copies, capacity, _ = copies_ref.shape
    rows = lax.broadcasted_iota(jnp.int32, (tokens, tokens), 0)
    columns = lax.broadcasted_iota(jnp.int32, (tokens, tokens), 1)
    before = jnp.where(rows < columns, 1.0, 0.0).astype(BF16)
    slot = lax.broadcasted_iota(jnp.int32, (capacity, tokens), 0).astype(F32)
    moves[0].wait()
    moves[1].wait()
    matches = ids_ref[...] == 0
    chosen = jnp.max(jnp.where(matches, 1.0, 0.0), axis=0, keepdims=True)
    weight = jnp.sum(jnp.where(matches, probs_ref[...], 0.0), axis=0, keepdims=True)
    chosen = jnp.broadcast_to(chosen, (capacity, tokens))
    earlier = dot(chosen.astype(BF16), before, PLAIN)
    placement = jnp.where((earlier == slot) & (chosen > 0.5), 1.0, 0.0)
    placement_ref[...] = placement.astype(BF16)
    scale = jnp.sum(placement * weight, axis=1, keepdims=True)
    moves[2].wait()
    picked = dot(placement.astype(BF16), grad_ref[...], PLAIN)
    outgoing = (picked * scale).astype(BF16)
    for i in range(copies):
        copies_ref[i] = outgoing
    for move in moves[3:]:
        move.wait()


def copies_kernel(value_ref, copies_ref):
    for i in range(copies_ref.shape[0]):
        copies_ref[i] = value_ref[...]


def pre_kernel(own_ref, across_ref, near_ref, diagonal_ref, saved_ref, gathered_ref, parts_ref, w_hbm, w_ref, sem):
    units = own_ref.shape[1]
    group = 4 * units
    for k in range(3):
        for i, ref in enumerate((own_ref, across_ref, near_ref, diagonal_ref)):
            w_ref[k * group + i * units : k * group + (i + 1) * units] = ref[k]
    store = pltpu.make_async_copy(w_ref.at[pl.ds(0, 2 * group)], w_hbm, sem.at[0])
    store.start()
    parts_ref[:, : 2 * group] = dot(saved_ref[...], w_ref[: 2 * group], LANES).astype(BF16)
    parts_ref[:, 2 * group :] = dot(gathered_ref[...], w_ref[2 * group :], LANES).astype(BF16)
    store.wait()


def activation_kernel(parts_ref, copies_ref):
    sources, _, wide = parts_ref.shape
    group = wide // 3
    total = parts_ref[0].astype(F32)
    for i in range(1, sources):
        total += parts_ref[i].astype(F32)
    gate_pre, up_pre, hid_grad = (total[:, k * group : (k + 1) * group] for k in range(3))
    sigmoid_gate = jax.nn.sigmoid(gate_pre)
    activated = gate_pre * sigmoid_gate
    gate_slope = sigmoid_gate + gate_pre * sigmoid_gate * (1.0 - sigmoid_gate)
    gate_grad = hid_grad * up_pre * gate_slope
    act = jnp.concatenate([gate_grad, hid_grad * activated, activated * up_pre], axis=1).astype(BF16)
    for i in range(sources):
        copies_ref[i] = act


def columns_of(act_ref, k, members):
    group = act_ref.shape[1] // 3
    units = group // 4
    return [act_ref[:, k * group + i * units : k * group + (i + 1) * units] for i in members]


def pack_kernel(act_ref, sent_ref):
    columns = [c for k in range(3) for c in columns_of(act_ref, k, (1, 3))]
    spare = sent_ref.shape[1] - act_ref.shape[1] // 2
    columns.append(jnp.zeros((act_ref.shape[0], spare), BF16))
    sent_ref[...] = jnp.concatenate(columns, axis=1)


def slot_kernel(act_ref, w_ref, slot_hbm, slot_ref, sems):
    stores = []
    rows = act_ref.shape[0] // N_YH
    for i in range(N_YH):
        block = pl.ds(i * rows, rows)
        slot_ref[block] = dot(act_ref[block, : w_ref.shape[0]], w_ref[...], PLAIN).astype(BF16)
        stores.append(pltpu.make_async_copy(slot_ref.at[block], slot_hbm.at[block], sems.at[i]))
        stores[-1].start()
    for store in stores:
        store.wait()


def near_kernel(act_ref, saved_ref, gathered_ref, part_ref):
    for k in range(3):
        here = gathered_ref if k == 2 else saved_ref
        part_ref[k] = dot(jnp.concatenate(columns_of(act_ref, k, (0, 2)), axis=1), here[...], ROWS)


def far_kernel(act_ref, saved_ref, gathered_ref, part_ref, own_ref, sent_ref):
    units = own_ref.shape[1]
    for k in range(3):
        far = gathered_ref if k == 2 else saved_ref
        part = part_ref[k] + dot(act_ref[:, 2 * k * units : 2 * (k + 1) * units], far[...], ROWS)
        own_ref[k] = part[:units]
        sent_ref[k] = part[units:].astype(BF16)


def sum_kernel(parts_ref, total_ref):
    total = parts_ref[0].astype(F32)
    for i in range(1, parts_ref.shape[0]):
        total += parts_ref[i].astype(F32)
    total_ref[...] = total.astype(BF16)


def result_kernel(parts_ref, placement_ref, grad_ref, result_ref):
    total = parts_ref[0].astype(F32)
    for i in range(1, parts_ref.shape[0]):
        total += parts_ref[i].astype(F32)
    routed = dot(placement_ref[...], total.astype(BF16), ROWS)
    result_ref[...] = (grad_ref[...].astype(F32) + routed).astype(BF16)


def local(grad_out, expert_ids, route_probs, saved_inputs, w_gate, w_up, w_down):
    tokens, width = grad_out.shape
    capacity = tokens // 8
    units = w_gate.shape[0]
    slots = N_FAR * capacity
    group = 4 * units

    copies, placement, own = pl.pallas_call(
        route_kernel,
        out_shape=[array(N_ZH, capacity, width), array(capacity, tokens), HBM((3, units, width), BF16)],
        in_specs=[pl.BlockSpec(memory_space=pl.ANY)] * 6,
        out_specs=[pl.BlockSpec(memory_space=VMEM)] * 3,
        scratch_shapes=[
            VMEM((tokens, width), BF16),
            VMEM(expert_ids.shape[::-1], jnp.int32),
            VMEM(route_probs.shape[::-1], F32),
            pltpu.SemaphoreType.DMA((6,)),
        ],
    )(grad_out, expert_ids.T, route_probs.T, w_gate, w_up, w_down)

    copies = lax.all_to_all(copies, "zh", 0, 0, tiled=True).reshape(N_ZH * capacity, width)
    copies, own = lax.optimization_barrier((copies, own))
    near = lax.ppermute(own, "core", SWAP)
    across = lax.ppermute(own, "zl", SWAP)
    (copies,) = kernel_call(copies_kernel, [HBM((N_YH, N_ZH * capacity, width), BF16)], 0, copies)
    diagonal = lax.ppermute(across, "core", SWAP)
    gathered = lax.all_to_all(copies, "yh", 0, 0, tiled=True).reshape(slots, width)

    def slots_of(member):
        rows = saved_inputs.reshape(N_FAR, 4, capacity, width)
        return lax.dynamic_index_in_dim(rows, member, axis=1, keepdims=False).reshape(slots, width)

    chip, core = lax.axis_index("zl"), lax.axis_index("core")
    saved = slots_of(chip * 2 + core)
    saved_far = slots_of((1 - chip) * 2 + core)

    pieces = (own, across, near, diagonal)
    parts, w_both = pl.pallas_call(
        pre_kernel,
        out_shape=[array(slots, 3 * group), HBM((2 * group, width), BF16)],
        in_specs=[pl.BlockSpec(memory_space=VMEM)] * 6,
        out_specs=[pl.BlockSpec(memory_space=VMEM), pl.BlockSpec(memory_space=pl.ANY)],
        scratch_shapes=[VMEM((3 * group, width), BF16), pltpu.SemaphoreType.DMA((1,))],
        cost_estimate=pl.CostEstimate(flops=6 * slots * group * width, bytes_accessed=4000000, transcendentals=0),
        compiler_params=pltpu.CompilerParams(vmem_limit_bytes=24 * 1024 * 1024),
    )(*pieces, saved, gathered)
    gathered_far = lax.ppermute(gathered, "zl", SWAP)
    parts = lax.all_to_all(parts.reshape(N_EP, slots // N_EP, 3 * group), EP, 0, 0, tiled=True)
    (copies,) = kernel_call(activation_kernel, [array(*parts.shape)], 20 * parts.size, parts)
    act = lax.all_to_all(copies, EP, 0, 0, tiled=True)
    act = act.reshape(slots, 3 * group)

    (sent,) = kernel_call(pack_kernel, [HBM((slots, width), BF16)], act.size, act)
    act_far = lax.ppermute(sent, "zl", SWAP)
    slot_part = pl.pallas_call(
        slot_kernel,
        out_shape=HBM((slots, width), BF16),
        in_specs=[pl.BlockSpec(memory_space=VMEM)] * 2,
        out_specs=pl.BlockSpec(memory_space=pl.ANY),
        scratch_shapes=[VMEM((slots, width), BF16), pltpu.SemaphoreType.DMA((N_YH,))],
        cost_estimate=pl.CostEstimate(flops=4 * slots * group * width, bytes_accessed=3000000, transcendentals=0),
        compiler_params=pltpu.CompilerParams(vmem_limit_bytes=24 * 1024 * 1024),
    )(act, w_both)

    slot_part = lax.all_to_all(slot_part.reshape(N_YH, N_ZH * capacity, width), "yh", 0, 0, tiled=True)
    (part,) = kernel_call(
        near_kernel, [array(3, 2 * units, width, dtype=F32)], 3 * slots * group * width, act, saved, gathered
    )
    kept, sent = kernel_call(
        far_kernel,
        [HBM((3, units, width), F32), HBM((3, units, width), BF16)],
        3 * slots * group * width,
        act_far,
        saved_far,
        gathered_far,
        part,
    )
    from_near = lax.ppermute(sent, "core", SWAP)
    (slot_part,) = kernel_call(sum_kernel, [HBM((N_ZH * capacity, width), BF16)], slot_part.size, slot_part)
    slot_part = lax.all_to_all(slot_part.reshape(N_ZH, capacity, width), "zh", 0, 0, tiled=True)
    (grad_in,) = kernel_call(result_kernel, [array(tokens, width)], tokens * width * 32, slot_part, placement, grad_out)

    grad_gate, grad_up, grad_down = [kept[k] + from_near[k].astype(F32) for k in range(3)]
    return (grad_in, grad_gate, grad_up, grad_down)


def solution(mesh):
    fine = Mesh(mesh.devices.reshape(SIZES), AXES)
    in_specs = (P(DP, EP), P(DP, None), P(DP, None), P(None, EP), P(DP, EP), P(DP, EP), P(DP, EP))
    return jax.shard_map(local, mesh=fine, in_specs=in_specs, out_specs=(P(DP, EP),) * 4, check_vma=False)
```

```python
import functools

import jax
import jax.numpy as jnp
from jax import lax
from jax.experimental import pallas as pl
from jax.experimental.pallas import tpu as pltpu
from jax.sharding import Mesh, PartitionSpec as P

AXES = ("yh", "zh", "zl", "core", "x", "yl")
SIZES = (4, 6, 2, 2, 4, 2)
DP = AXES[:4]
EP = AXES[4:]
N_YH = 4
N_ZH = 6
N_FAR = 24
N_EP = 8
SWAP = [(0, 1), (1, 0)]
BF16 = jnp.bfloat16
F32 = jnp.float32


VMEM = pltpu.VMEM
HBM = pltpu.HBM


def kernel_call(body, outs, flops, *args):
    moved = sum(a.size * a.dtype.itemsize for a in args)
    return pl.pallas_call(
        body,
        out_shape=outs,
        in_specs=[pl.BlockSpec(memory_space=VMEM)] * len(args),
        out_specs=[pl.BlockSpec(memory_space=VMEM)] * len(outs),
        cost_estimate=pl.CostEstimate(flops=flops, bytes_accessed=moved, transcendentals=0),
        compiler_params=pltpu.CompilerParams(vmem_limit_bytes=24 * 1024 * 1024),
    )(*args)


def array(*shape, dtype=BF16):
    return jax.ShapeDtypeStruct(shape, dtype)


def dot(a, b, dims):
    return lax.dot_general(a, b, (dims, ((), ())), preferred_element_type=F32)


ROWS = ((0,), (0,))
PLAIN = ((1,), (0,))
LANES = ((1,), (1,))


def route_kernel(
    grad_hbm, ids_hbm, probs_hbm, wg_hbm, wu_hbm, wd_hbm, copies_ref, placement_ref, own_ref, grad_ref, ids_ref, probs_ref, sems
):
    pairs = (
        (ids_hbm, ids_ref),
        (probs_hbm, probs_ref),
        (grad_hbm, grad_ref),
        (wg_hbm, own_ref.at[0]),
        (wu_hbm, own_ref.at[1]),
        (wd_hbm, own_ref.at[2]),
    )
    moves = [pltpu.make_async_copy(a, b, sems.at[i]) for i, (a, b) in enumerate(pairs)]
    for move in moves:
        move.start()
    tokens = grad_ref.shape[0]
    copies, capacity, _ = copies_ref.shape
    rows = lax.broadcasted_iota(jnp.int32, (tokens, tokens), 0)
    columns = lax.broadcasted_iota(jnp.int32, (tokens, tokens), 1)
    before = jnp.where(rows < columns, 1.0, 0.0).astype(BF16)
    slot = lax.broadcasted_iota(jnp.int32, (capacity, tokens), 0).astype(F32)
    moves[0].wait()
    moves[1].wait()
    matches = ids_ref[...] == 0
    chosen = jnp.max(jnp.where(matches, 1.0, 0.0), axis=0, keepdims=True)
    weight = jnp.sum(jnp.where(matches, probs_ref[...], 0.0), axis=0, keepdims=True)
    chosen = jnp.broadcast_to(chosen, (capacity, tokens))
    earlier = dot(chosen.astype(BF16), before, PLAIN)
    placement = jnp.where((earlier == slot) & (chosen > 0.5), 1.0, 0.0)
    placement_ref[...] = placement.astype(BF16)
    scale = jnp.sum(placement * weight, axis=1, keepdims=True)
    moves[2].wait()
    picked = dot(placement.astype(BF16), grad_ref[...], PLAIN)
    outgoing = (picked * scale).astype(BF16)
    for i in range(copies):
        copies_ref[i] = outgoing
    for move in moves[3:]:
        move.wait()


def copies_kernel(value_ref, copies_ref):
    for i in range(copies_ref.shape[0]):
        copies_ref[i] = value_ref[...]


def pre_kernel(own_ref, across_ref, near_ref, diagonal_ref, saved_ref, gathered_ref, parts_ref, w_ref):
    units = own_ref.shape[1]
    group = 4 * units
    for k in range(3):
        for i, ref in enumerate((own_ref, across_ref, near_ref, diagonal_ref)):
            w_ref[k * group + i * units : k * group + (i + 1) * units] = ref[k]
    parts_ref[:, : 2 * group] = dot(saved_ref[...], w_ref[: 2 * group], LANES).astype(BF16)
    parts_ref[:, 2 * group :] = dot(gathered_ref[...], w_ref[2 * group :], LANES).astype(BF16)


def weights_kernel(own_ref, across_ref, near_ref, diagonal_ref, w_ref):
    units = own_ref.shape[1]
    for k in range(2):
        for i, ref in enumerate((own_ref, across_ref, near_ref, diagonal_ref)):
            w_ref[(4 * k + i) * units : (4 * k + i + 1) * units] = ref[k]


def activation_kernel(parts_ref, copies_ref):
    sources, _, wide = parts_ref.shape
    group = wide // 3
    total = parts_ref[0].astype(F32)
    for i in range(1, sources):
        total += parts_ref[i].astype(F32)
    gate_pre, up_pre, hid_grad = (total[:, k * group : (k + 1) * group] for k in range(3))
    sigmoid_gate = jax.nn.sigmoid(gate_pre)
    activated = gate_pre * sigmoid_gate
    gate_slope = sigmoid_gate + gate_pre * sigmoid_gate * (1.0 - sigmoid_gate)
    gate_grad = hid_grad * up_pre * gate_slope
    act = jnp.concatenate([gate_grad, hid_grad * activated, activated * up_pre], axis=1).astype(BF16)
    for i in range(sources):
        copies_ref[i] = act


def columns_of(act_ref, k, members):
    group = act_ref.shape[1] // 3
    units = group // 4
    return [act_ref[:, k * group + i * units : k * group + (i + 1) * units] for i in members]


def pack_kernel(act_ref, sent_ref):
    columns = [c for k in range(3) for c in columns_of(act_ref, k, (1, 3))]
    spare = sent_ref.shape[1] - act_ref.shape[1] // 2
    columns.append(jnp.zeros((act_ref.shape[0], spare), BF16))
    sent_ref[...] = jnp.concatenate(columns, axis=1)


def slot_kernel(act_ref, w_ref, slot_hbm, slot_ref, sems):
    stores = []
    rows = act_ref.shape[0] // N_YH
    for i in range(N_YH):
        block = pl.ds(i * rows, rows)
        slot_ref[block] = dot(act_ref[block, : w_ref.shape[0]], w_ref[...], PLAIN).astype(BF16)
        stores.append(pltpu.make_async_copy(slot_ref.at[block], slot_hbm.at[block], sems.at[i]))
        stores[-1].start()
    for store in stores:
        store.wait()


def near_kernel(act_ref, saved_ref, gathered_ref, part_ref):
    for k in range(3):
        here = gathered_ref if k == 2 else saved_ref
        part_ref[k] = dot(jnp.concatenate(columns_of(act_ref, k, (0, 2)), axis=1), here[...], ROWS)


def far_kernel(act_ref, saved_ref, gathered_ref, part_ref, own_ref, sent_ref):
    units = own_ref.shape[1]
    for k in range(3):
        far = gathered_ref if k == 2 else saved_ref
        part = part_ref[k] + dot(act_ref[:, 2 * k * units : 2 * (k + 1) * units], far[...], ROWS)
        own_ref[k] = part[:units]
        sent_ref[k] = part[units:].astype(BF16)


def sum_kernel(parts_ref, total_ref):
    total = parts_ref[0].astype(F32)
    for i in range(1, parts_ref.shape[0]):
        total += parts_ref[i].astype(F32)
    total_ref[...] = total.astype(BF16)


def result_kernel(parts_ref, placement_ref, grad_ref, result_ref):
    total = parts_ref[0].astype(F32)
    for i in range(1, parts_ref.shape[0]):
        total += parts_ref[i].astype(F32)
    routed = dot(placement_ref[...], total.astype(BF16), ROWS)
    result_ref[...] = (grad_ref[...].astype(F32) + routed).astype(BF16)


def local(grad_out, expert_ids, route_probs, saved_inputs, w_gate, w_up, w_down):
    tokens, width = grad_out.shape
    capacity = tokens // 8
    units = w_gate.shape[0]
    slots = N_FAR * capacity
    group = 4 * units

    copies, placement, own = pl.pallas_call(
        route_kernel,
        out_shape=[array(N_ZH, capacity, width), array(capacity, tokens), HBM((3, units, width), BF16)],
        in_specs=[pl.BlockSpec(memory_space=pl.ANY)] * 6,
        out_specs=[pl.BlockSpec(memory_space=VMEM)] * 3,
        scratch_shapes=[
            VMEM((tokens, width), BF16),
            VMEM(expert_ids.shape[::-1], jnp.int32),
            VMEM(route_probs.shape[::-1], F32),
            pltpu.SemaphoreType.DMA((6,)),
        ],
    )(grad_out, expert_ids.T, route_probs.T, w_gate, w_up, w_down)

    copies = lax.all_to_all(copies, "zh", 0, 0, tiled=True).reshape(N_ZH * capacity, width)
    copies, own = lax.optimization_barrier((copies, own))
    near = lax.ppermute(own, "core", SWAP)
    across = lax.ppermute(own, "zl", SWAP)
    (copies,) = kernel_call(copies_kernel, [HBM((N_YH, N_ZH * capacity, width), BF16)], 0, copies)
    diagonal = lax.ppermute(across, "core", SWAP)
    gathered = lax.all_to_all(copies, "yh", 0, 0, tiled=True).reshape(slots, width)

    def slots_of(member):
        rows = saved_inputs.reshape(N_FAR, 4, capacity, width)
        return lax.dynamic_index_in_dim(rows, member, axis=1, keepdims=False).reshape(slots, width)

    chip, core = lax.axis_index("zl"), lax.axis_index("core")
    saved = slots_of(chip * 2 + core)
    saved_far = slots_of((1 - chip) * 2 + core)

    pieces = (own, across, near, diagonal)
    (parts,) = pl.pallas_call(
        pre_kernel,
        out_shape=[array(slots, 3 * group)],
        in_specs=[pl.BlockSpec(memory_space=VMEM)] * 6,
        out_specs=[pl.BlockSpec(memory_space=VMEM)],
        scratch_shapes=[VMEM((3 * group, width), BF16)],
        cost_estimate=pl.CostEstimate(flops=6 * slots * group * width, bytes_accessed=4000000, transcendentals=0),
        compiler_params=pltpu.CompilerParams(vmem_limit_bytes=24 * 1024 * 1024),
    )(*pieces, saved, gathered)
    gathered_far = lax.ppermute(gathered, "zl", SWAP)
    parts = lax.all_to_all(parts.reshape(N_EP, slots // N_EP, 3 * group), EP, 0, 0, tiled=True)
    parts, pieces = lax.optimization_barrier((parts, pieces))
    (w_both,) = kernel_call(weights_kernel, [array(2 * group, width)], 1000000, *pieces)
    (copies,) = kernel_call(activation_kernel, [array(*parts.shape)], 20 * parts.size, parts)
    act = lax.all_to_all(copies, EP, 0, 0, tiled=True)
    act = act.reshape(slots, 3 * group)

    (sent,) = kernel_call(pack_kernel, [HBM((slots, width), BF16)], act.size, act)
    act_far = lax.ppermute(sent, "zl", SWAP)
    slot_part = pl.pallas_call(
        slot_kernel,
        out_shape=HBM((slots, width), BF16),
        in_specs=[pl.BlockSpec(memory_space=VMEM)] * 2,
        out_specs=pl.BlockSpec(memory_space=pl.ANY),
        scratch_shapes=[VMEM((slots, width), BF16), pltpu.SemaphoreType.DMA((N_YH,))],
        cost_estimate=pl.CostEstimate(flops=4 * slots * group * width, bytes_accessed=3000000, transcendentals=0),
        compiler_params=pltpu.CompilerParams(vmem_limit_bytes=24 * 1024 * 1024),
    )(act, w_both)

    slot_part = lax.all_to_all(slot_part.reshape(N_YH, N_ZH * capacity, width), "yh", 0, 0, tiled=True)
    (part,) = kernel_call(
        near_kernel, [array(3, 2 * units, width, dtype=F32)], 3 * slots * group * width, act, saved, gathered
    )
    kept, sent = kernel_call(
        far_kernel,
        [HBM((3, units, width), F32), HBM((3, units, width), BF16)],
        3 * slots * group * width,
        act_far,
        saved_far,
        gathered_far,
        part,
    )
    from_near = lax.ppermute(sent, "core", SWAP)
    (slot_part,) = kernel_call(sum_kernel, [HBM((N_ZH * capacity, width), BF16)], slot_part.size, slot_part)
    slot_part = lax.all_to_all(slot_part.reshape(N_ZH, capacity, width), "zh", 0, 0, tiled=True)
    (grad_in,) = kernel_call(result_kernel, [array(tokens, width)], tokens * width * 32, slot_part, placement, grad_out)

    grad_gate, grad_up, grad_down = [kept[k] + from_near[k].astype(F32) for k in range(3)]
    return (grad_in, grad_gate, grad_up, grad_down)


def solution(mesh):
    fine = Mesh(mesh.devices.reshape(SIZES), AXES)
    in_specs = (P(DP, EP), P(DP, None), P(DP, None), P(None, EP), P(DP, EP), P(DP, EP), P(DP, EP))
    return jax.shard_map(local, mesh=fine, in_specs=in_specs, out_specs=(P(DP, EP),) * 4, check_vma=False)
```

```python
import functools

import jax
import jax.numpy as jnp
from jax import lax
from jax.experimental import pallas as pl
from jax.experimental.pallas import tpu as pltpu
from jax.sharding import Mesh, PartitionSpec as P

AXES = ("yh", "zh", "zl", "core", "x", "yl")
SIZES = (4, 6, 2, 2, 4, 2)
DP = AXES[:4]
EP = AXES[4:]
N_YH = 4
N_ZH = 6
N_FAR = 24
N_EP = 8
SWAP = [(0, 1), (1, 0)]
BF16 = jnp.bfloat16
F32 = jnp.float32


VMEM = pltpu.VMEM
HBM = pltpu.HBM


def kernel_call(body, outs, flops, *args):
    moved = sum(a.size * a.dtype.itemsize for a in args)
    return pl.pallas_call(
        body,
        out_shape=outs,
        in_specs=[pl.BlockSpec(memory_space=VMEM)] * len(args),
        out_specs=[pl.BlockSpec(memory_space=VMEM)] * len(outs),
        cost_estimate=pl.CostEstimate(flops=flops, bytes_accessed=moved, transcendentals=0),
        compiler_params=pltpu.CompilerParams(vmem_limit_bytes=24 * 1024 * 1024),
    )(*args)


def array(*shape, dtype=BF16):
    return jax.ShapeDtypeStruct(shape, dtype)


def dot(a, b, dims):
    return lax.dot_general(a, b, (dims, ((), ())), preferred_element_type=F32)


ROWS = ((0,), (0,))
PLAIN = ((1,), (0,))
LANES = ((1,), (1,))


def route_kernel(
    grad_hbm, ids_hbm, probs_hbm, wg_hbm, wu_hbm, wd_hbm, copies_ref, placement_ref, own_ref, grad_ref, ids_ref, probs_ref, sems
):
    pairs = (
        (ids_hbm, ids_ref),
        (probs_hbm, probs_ref),
        (grad_hbm, grad_ref),
        (wg_hbm, own_ref.at[0]),
        (wu_hbm, own_ref.at[1]),
        (wd_hbm, own_ref.at[2]),
    )
    moves = [pltpu.make_async_copy(a, b, sems.at[i]) for i, (a, b) in enumerate(pairs)]
    for move in moves:
        move.start()
    tokens = grad_ref.shape[0]
    copies, capacity, _ = copies_ref.shape
    rows = lax.broadcasted_iota(jnp.int32, (tokens, tokens), 0)
    columns = lax.broadcasted_iota(jnp.int32, (tokens, tokens), 1)
    before = jnp.where(rows < columns, 1.0, 0.0).astype(BF16)
    slot = lax.broadcasted_iota(jnp.int32, (capacity, tokens), 0).astype(F32)
    moves[0].wait()
    moves[1].wait()
    matches = ids_ref[...] == 0
    chosen = jnp.max(jnp.where(matches, 1.0, 0.0), axis=0, keepdims=True)
    weight = jnp.sum(jnp.where(matches, probs_ref[...], 0.0), axis=0, keepdims=True)
    chosen = jnp.broadcast_to(chosen, (capacity, tokens))
    earlier = dot(chosen.astype(BF16), before, PLAIN)
    placement = jnp.where((earlier == slot) & (chosen > 0.5), 1.0, 0.0)
    placement_ref[...] = placement.astype(BF16)
    scale = jnp.sum(placement * weight, axis=1, keepdims=True)
    moves[2].wait()
    picked = dot(placement.astype(BF16), grad_ref[...], PLAIN)
    outgoing = (picked * scale).astype(BF16)
    for i in range(copies):
        copies_ref[i] = outgoing
    for move in moves[3:]:
        move.wait()


def copies_kernel(value_ref, copies_ref):
    for i in range(copies_ref.shape[0]):
        copies_ref[i] = value_ref[...]


def pre_kernel(own_ref, across_ref, near_ref, diagonal_ref, saved_ref, gathered_ref, parts_ref, w_ref):
    units = own_ref.shape[1]
    group = 4 * units
    for k in range(3):
        for i, ref in enumerate((own_ref, across_ref, near_ref, diagonal_ref)):
            w_ref[k * group + i * units : k * group + (i + 1) * units] = ref[k]
    parts_ref[:, : 2 * group] = dot(saved_ref[...], w_ref[: 2 * group], LANES).astype(BF16)
    parts_ref[:, 2 * group :] = dot(gathered_ref[...], w_ref[2 * group :], LANES).astype(BF16)


def weights_kernel(own_ref, across_ref, near_ref, diagonal_ref, w_ref):
    units = own_ref.shape[1]
    for k in range(2):
        for i, ref in enumerate((own_ref, across_ref, near_ref, diagonal_ref)):
            w_ref[(4 * k + i) * units : (4 * k + i + 1) * units] = ref[k]


def activation_kernel(parts_ref, copies_ref):
    sources, _, wide = parts_ref.shape
    group = wide // 3
    total = parts_ref[0].astype(F32)
    for i in range(1, sources):
        total += parts_ref[i].astype(F32)
    gate_pre, up_pre, hid_grad = (total[:, k * group : (k + 1) * group] for k in range(3))
    sigmoid_gate = jax.nn.sigmoid(gate_pre)
    activated = gate_pre * sigmoid_gate
    gate_slope = sigmoid_gate + gate_pre * sigmoid_gate * (1.0 - sigmoid_gate)
    gate_grad = hid_grad * up_pre * gate_slope
    act = jnp.concatenate([gate_grad, hid_grad * activated, activated * up_pre], axis=1).astype(BF16)
    for i in range(sources):
        copies_ref[i] = act


def columns_of(act_ref, k, members):
    group = act_ref.shape[1] // 3
    units = group // 4
    return [act_ref[:, k * group + i * units : k * group + (i + 1) * units] for i in members]


def pack_kernel(act_ref, sent_ref):
    columns = [c for k in range(3) for c in columns_of(act_ref, k, (1, 3))]
    spare = sent_ref.shape[1] - act_ref.shape[1] // 2
    columns.append(jnp.zeros((act_ref.shape[0], spare), BF16))
    sent_ref[...] = jnp.concatenate(columns, axis=1)


def slot_kernel(act_ref, own_ref, across_ref, near_ref, diagonal_ref, slot_hbm, w_ref, slot_ref, sems):
    weights_kernel(own_ref, across_ref, near_ref, diagonal_ref, w_ref)
    stores = []
    rows = act_ref.shape[0] // N_YH
    for i in range(N_YH):
        block = pl.ds(i * rows, rows)
        slot_ref[block] = dot(act_ref[block, : w_ref.shape[0]], w_ref[...], PLAIN).astype(BF16)
        stores.append(pltpu.make_async_copy(slot_ref.at[block], slot_hbm.at[block], sems.at[i]))
        stores[-1].start()
    for store in stores:
        store.wait()


def near_kernel(act_ref, saved_ref, gathered_ref, part_ref):
    for k in range(3):
        here = gathered_ref if k == 2 else saved_ref
        part_ref[k] = dot(jnp.concatenate(columns_of(act_ref, k, (0, 2)), axis=1), here[...], ROWS)


def far_kernel(act_ref, saved_ref, gathered_ref, part_ref, own_ref, sent_ref):
    units = own_ref.shape[1]
    for k in range(3):
        far = gathered_ref if k == 2 else saved_ref
        part = part_ref[k] + dot(act_ref[:, 2 * k * units : 2 * (k + 1) * units], far[...], ROWS)
        own_ref[k] = part[:units]
        sent_ref[k] = part[units:].astype(BF16)


def sum_kernel(parts_ref, total_ref):
    total = parts_ref[0].astype(F32)
    for i in range(1, parts_ref.shape[0]):
        total += parts_ref[i].astype(F32)
    total_ref[...] = total.astype(BF16)


def result_kernel(parts_ref, placement_ref, grad_ref, result_ref):
    total = parts_ref[0].astype(F32)
    for i in range(1, parts_ref.shape[0]):
        total += parts_ref[i].astype(F32)
    routed = dot(placement_ref[...], total.astype(BF16), ROWS)
    result_ref[...] = (grad_ref[...].astype(F32) + routed).astype(BF16)


def local(grad_out, expert_ids, route_probs, saved_inputs, w_gate, w_up, w_down):
    tokens, width = grad_out.shape
    capacity = tokens // 8
    units = w_gate.shape[0]
    slots = N_FAR * capacity
    group = 4 * units

    copies, placement, own = pl.pallas_call(
        route_kernel,
        out_shape=[array(N_ZH, capacity, width), array(capacity, tokens), HBM((3, units, width), BF16)],
        in_specs=[pl.BlockSpec(memory_space=pl.ANY)] * 6,
        out_specs=[pl.BlockSpec(memory_space=VMEM)] * 3,
        scratch_shapes=[
            VMEM((tokens, width), BF16),
            VMEM(expert_ids.shape[::-1], jnp.int32),
            VMEM(route_probs.shape[::-1], F32),
            pltpu.SemaphoreType.DMA((6,)),
        ],
    )(grad_out, expert_ids.T, route_probs.T, w_gate, w_up, w_down)

    copies = lax.all_to_all(copies, "zh", 0, 0, tiled=True).reshape(N_ZH * capacity, width)
    copies, own = lax.optimization_barrier((copies, own))
    near = lax.ppermute(own, "core", SWAP)
    across = lax.ppermute(own, "zl", SWAP)
    (copies,) = kernel_call(copies_kernel, [HBM((N_YH, N_ZH * capacity, width), BF16)], 0, copies)
    diagonal = lax.ppermute(across, "core", SWAP)
    gathered = lax.all_to_all(copies, "yh", 0, 0, tiled=True).reshape(slots, width)

    def slots_of(member):
        rows = saved_inputs.reshape(N_FAR, 4, capacity, width)
        return lax.dynamic_index_in_dim(rows, member, axis=1, keepdims=False).reshape(slots, width)

    chip, core = lax.axis_index("zl"), lax.axis_index("core")
    saved = slots_of(chip * 2 + core)
    saved_far = slots_of((1 - chip) * 2 + core)

    pieces = (own, across, near, diagonal)
    (parts,) = pl.pallas_call(
        pre_kernel,
        out_shape=[array(slots, 3 * group)],
        in_specs=[pl.BlockSpec(memory_space=VMEM)] * 6,
        out_specs=[pl.BlockSpec(memory_space=VMEM)],
        scratch_shapes=[VMEM((3 * group, width), BF16)],
        cost_estimate=pl.CostEstimate(flops=6 * slots * group * width, bytes_accessed=4000000, transcendentals=0),
        compiler_params=pltpu.CompilerParams(vmem_limit_bytes=24 * 1024 * 1024),
    )(*pieces, saved, gathered)
    gathered_far = lax.ppermute(gathered, "zl", SWAP)
    parts = lax.all_to_all(parts.reshape(N_EP, slots // N_EP, 3 * group), EP, 0, 0, tiled=True)
    parts, pieces = lax.optimization_barrier((parts, pieces))
    (copies,) = kernel_call(activation_kernel, [array(*parts.shape)], 20 * parts.size, parts)
    act = lax.all_to_all(copies, EP, 0, 0, tiled=True)
    act = act.reshape(slots, 3 * group)

    (sent,) = kernel_call(pack_kernel, [HBM((slots, width), BF16)], act.size, act)
    act_far = lax.ppermute(sent, "zl", SWAP)
    slot_part = pl.pallas_call(
        slot_kernel,
        out_shape=HBM((slots, width), BF16),
        in_specs=[pl.BlockSpec(memory_space=VMEM)] * 5,
        out_specs=pl.BlockSpec(memory_space=pl.ANY),
        scratch_shapes=[VMEM((2 * group, width), BF16), VMEM((slots, width), BF16), pltpu.SemaphoreType.DMA((N_YH,))],
        cost_estimate=pl.CostEstimate(flops=4 * slots * group * width, bytes_accessed=3000000, transcendentals=0),
        compiler_params=pltpu.CompilerParams(vmem_limit_bytes=24 * 1024 * 1024),
    )(act, *pieces)

    slot_part = lax.all_to_all(slot_part.reshape(N_YH, N_ZH * capacity, width), "yh", 0, 0, tiled=True)
    (part,) = kernel_call(
        near_kernel, [array(3, 2 * units, width, dtype=F32)], 3 * slots * group * width, act, saved, gathered
    )
    kept, sent = kernel_call(
        far_kernel,
        [HBM((3, units, width), F32), HBM((3, units, width), BF16)],
        3 * slots * group * width,
        act_far,
        saved_far,
        gathered_far,
        part,
    )
    from_near = lax.ppermute(sent, "core", SWAP)
    (slot_part,) = kernel_call(sum_kernel, [HBM((N_ZH * capacity, width), BF16)], slot_part.size, slot_part)
    slot_part = lax.all_to_all(slot_part.reshape(N_ZH, capacity, width), "zh", 0, 0, tiled=True)
    (grad_in,) = kernel_call(result_kernel, [array(tokens, width)], tokens * width * 32, slot_part, placement, grad_out)

    grad_gate, grad_up, grad_down = [kept[k] + from_near[k].astype(F32) for k in range(3)]
    return (grad_in, grad_gate, grad_up, grad_down)


def solution(mesh):
    fine = Mesh(mesh.devices.reshape(SIZES), AXES)
    in_specs = (P(DP, EP), P(DP, None), P(DP, None), P(None, EP), P(DP, EP), P(DP, EP), P(DP, EP))
    return jax.shard_map(local, mesh=fine, in_specs=in_specs, out_specs=(P(DP, EP),) * 4, check_vma=False)
```
